256 devices in a mesh: dp: 16 (over y, x), row: 2 (over core), col: 8 (over z).
Axes of the slice: x: 4, y: 4, z: 8, core: 2. Of those that a mesh axis runs over, the one named last changes fastest.
Arguments:
- grads: bfloat16 [16, 3072, 8192], P('dp', 'row', 'col'), may hold values from -6 to 6
- errors: bfloat16 [16, 3072, 8192], P('dp', 'row', 'col'), may hold values from -4 to 4
- q_init: float32 [8192, 64], P('col'), may hold values from -6 to 6
Outputs:
- new_errors: bfloat16 [16, 3072, 8192], P('dp', 'row', 'col')
- q_factor: float32 [8192, 64], P('col')
The draws below stay inside these ranges and needn't reach their ends.
All inputs are finite; a program needn't handle non-finite values.
Results may differ from the reference program's by a relative error of at most 0.009.
Values may be sent and summed in bfloat16 or wider, within the bound.
A program may use at most 128 MiB of HBM per device.

```python
import jax
import jax.numpy as jnp
from jax import lax

RANK = 64
ITERS = 7
REPLICAS = 16
ROWS = 3072
COLS = 8192
N_DP = 16


def level_of(own_key, dims, cuts, low, largest):
    loudness = 1.0
    for dim, parts in cuts:
        steps = jax.random.uniform(jax.random.fold_in(jax.random.fold_in(own_key, 6), dim), (parts,), jnp.float32, low / len(cuts), largest / len(cuts))
        loudness = loudness * jnp.repeat(jnp.exp(steps), dims[dim] // parts).reshape((-1,) + (1,) * (len(dims) - 1 - dim))
    return loudness


def scatter_about(stream_key, shape, scale, most, shards=(), kind=jnp.bfloat16):
    result = scale * jax.random.normal(stream_key, shape, jnp.float32)
    if shards:
        result = result * level_of(stream_key, shape, shards, -0.22, 0.18)
    return jnp.clip(result, -most, most).astype(kind)


def setup_inputs(seed: int = 0) -> dict:
    streams_of = jax.random.split(jax.random.key(seed), 4)
    grads = scatter_about(streams_of[0], (REPLICAS, ROWS, COLS), 1.0, 6.0, ((0, 16), (1, 2), (2, 8)))
    errors = scatter_about(streams_of[1], (REPLICAS, ROWS, COLS), 0.5, 4.0, ((0, 16), (1, 2), (2, 8)))
    q_init = scatter_about(streams_of[2], (COLS, RANK), 1.0, 6.0, ((0, 8),), jnp.float32)
    return {"grads": grads, "errors": errors, "q_init": q_init}


def orthonormal(left, gram):
    lower = jnp.linalg.cholesky(gram)
    return lax.linalg.triangular_solve(lower, left, left_side=False, lower=True, transpose_a=True)

def reference(grads, errors, q_init):
    merged = lax.map(lambda pair: (pair[0].astype(jnp.float32) + pair[1].astype(jnp.float32)).astype(jnp.bfloat16), (grads, errors))
    q_now = q_init
    p_low = None
    for step in range(ITERS):
        q_low = q_now.astype(jnp.bfloat16)

        def add_left(total, matrix):
            return (total + jnp.dot(matrix.astype(jnp.float32), q_low.astype(jnp.float32), preferred_element_type=jnp.float32), None)
        total = lax.scan(add_left, jnp.zeros((ROWS, RANK), jnp.float32), merged)[0] / N_DP
        gram = jnp.dot(total.T, total, precision=lax.Precision.HIGHEST)
        basis = orthonormal(total, gram)
        p_low = basis.astype(jnp.bfloat16)

        def add_right(total, matrix):
            return (total + lax.dot_general(matrix.astype(jnp.float32), p_low.astype(jnp.float32), (((0,), (0,)), ((), ())), preferred_element_type=jnp.float32), None)
        q_now = lax.scan(add_right, jnp.zeros((COLS, RANK), jnp.float32), merged)[0] / N_DP
    approx = jnp.dot(p_low.astype(jnp.float32), q_now.astype(jnp.bfloat16).T.astype(jnp.float32), preferred_element_type=jnp.float32)
    new_errors = lax.map(lambda matrix: (matrix.astype(jnp.float32) - approx).astype(jnp.bfloat16), merged)
    return (new_errors, q_now)
```

```python
import functools

import jax
import jax.numpy as jnp
from jax import lax
from jax.experimental import pallas as pl
from jax.experimental.pallas import tpu as pltpu
from jax.sharding import PartitionSpec as P

MESH = pl.DeviceIdType.MESH
ITERS = 7
F32, BF16 = jnp.float32, jnp.bfloat16
NT = (((1,), (1,)), ((), ()))
TN = (((0,), (0,)), ((), ()))
SIDE = 4


def lanes(shape):
    return lax.broadcasted_iota(jnp.int32, shape, 1)


def halves(x):
    high = x.astype(BF16)
    low = (x - high.astype(F32)).astype(BF16)
    return jnp.where(lanes(x.shape) < 64, high, low)


def fold(x):
    return x + pltpu.roll(x, 64, 1)


def inverse_factor(gram):
    shape = (64, 128)
    lane, row = lanes(shape), lax.broadcasted_iota(jnp.int32, shape, 0)
    w = jnp.where(lane < 64, gram, (lane - 64 == row).astype(F32))
    for j in range(64):
        g = 8 * (j // 8)
        tail = w[g:]
        scale = tail[:, j : j + 1] * (1.0 / w[j : j + 1, j : j + 1])
        scale = jnp.where(row[g:, :1] > j, scale, 0.0)
        tail = tail - scale * w[j : j + 1]
        w = jnp.concatenate([w[:g], tail], 0) if g else tail
    pivot = jnp.sum(jnp.where(lane == row, w, 0.0), axis=1, keepdims=True)
    w = jnp.where(lane < 64, 0.0, w * lax.rsqrt(pivot))
    w = fold(w)
    high = w.astype(BF16)
    low = (w - high.astype(F32)).astype(BF16)
    both = jnp.concatenate([high, low], 1)
    return jnp.concatenate([both, both], 0)


def kernel(
    replicas, planes, g_ref, e_ref, q_ref, err_ref, qf_ref,
    g_buf, e_buf, merged, rs_buf, mz, own, kpart, kfull, zbuf, zp, zp_own, v, pp, factor, ysend, yrecv, gsend, grecv,
    qsend, qrecv, qlow, plow, out_buf,
    g_sem, e_sem, rs_s, rs_r, ag_s, ag_r, own_sem, z1_s, z1_r, z2_s, z2_r, z3_s, z3_r, it_s, it_r, y_sem, gr_sem, q_sem, o_sem,
):
    dp, core, z = lax.axis_index("dp"), lax.axis_index("row"), lax.axis_index("col")
    y, x = dp // SIDE, dp % SIDE
    rows, cols = merged.shape
    part = rows // replicas
    half = kfull.shape[1] // 2
    quarter = kfull.shape[0] // 4

    def peer(i):
        return ((y + i // SIDE) % SIDE) * SIDE + (x + i % SIDE) % SIDE

    def source(i):
        return ((y + SIDE - i // SIDE) % SIDE) * SIDE + (x + SIDE - i % SIDE) % SIDE

    def at(i):
        return pl.ds(pl.multiple_of(i * part, part), part)

    def zpeer(i):
        return (z + i) % planes

    def zsource(i):
        return (z + planes - i) % planes

    def remote(src, dst, ssem, rsem, **device):
        return pltpu.make_async_remote_copy(
            src_ref=src, dst_ref=dst, send_sem=ssem, recv_sem=rsem, device_id=device, device_id_type=MESH
        )

    def each(lo, hi, body):
        def step(i, carry):
            body(i)
            return carry

        lax.fori_loop(lo, hi, step, 0)

    def load(i):
        here = at(peer(i))
        pltpu.make_async_copy(g_ref.at[0, here], g_buf.at[here], g_sem.at[i]).start()
        pltpu.make_async_copy(e_ref.at[0, here], e_buf.at[here], e_sem.at[i]).start()

    each(0, replicas, load)
    barrier = pltpu.get_barrier_semaphore()
    each(1, replicas, lambda i: pl.semaphore_signal(barrier, inc=1, device_id={"dp": peer(i)}, device_id_type=MESH))
    each(1, planes, lambda i: pl.semaphore_signal(barrier, inc=1, device_id={"col": zpeer(i)}, device_id_type=MESH))
    pl.semaphore_signal(barrier, inc=1, device_id={"row": 1 - core}, device_id_type=MESH)
    pl.semaphore_wait(barrier, replicas - 1 + planes - 1 + 1)

    def scatter(i):
        return remote(merged.at[at(peer(i))], rs_buf.at[i], rs_s.at[i], rs_r.at[i], dp=peer(i))

    def merge(i):
        here = at(peer(i))
        pltpu.make_async_copy(g_ref.at[0, here], g_buf.at[here], g_sem.at[i]).wait()
        pltpu.make_async_copy(e_ref.at[0, here], e_buf.at[here], e_sem.at[i]).wait()
        merged[here, :] = (g_buf[here, :].astype(F32) + e_buf[here, :].astype(F32)).astype(BF16)

    def merge_send(i):
        merge(i)
        scatter(i).start()

    each(1, replicas, merge_send)
    merge(0)
    each(1, replicas, lambda i: scatter(i).wait_recv())

    def mean(i):
        sub = pl.ds(pl.multiple_of(i * 16, 16), 16)
        total = merged[pl.ds(pl.multiple_of(dp * part + i * 16, 16), 16), :].astype(F32)
        for r in range(1, replicas):
            total = total + rs_buf[r, sub, :].astype(F32)
        low = (total * (1.0 / replicas)).astype(BF16)
        mz[pl.ds(pl.multiple_of(dp * part + i * 16, 16), 16), :] = low
        own[core, sub, :] = low

    each(0, part // 16, mean)

    def gather(i, owner):
        return remote(mz.at[at(owner)], mz.at[at(owner)], ag_s.at[i], ag_r.at[i], dp=peer(i))

    swap_own = remote(own.at[core], own.at[core], own_sem.at[0], own_sem.at[1], row=1 - core)
    each(1, replicas, lambda i: gather(i, dp).start())
    swap_own.start()

    first = jnp.dot(own[core], q_ref[...].astype(BF16), preferred_element_type=F32)
    zp_own[...] = halves(jnp.concatenate([first, first], 1))

    def first_sum(i):
        return remote(zp_own, zp.at[i], z1_s.at[i], z1_r.at[i], col=zpeer(i))

    each(1, planes, lambda i: first_sum(i).start())
    each(1, planes, lambda i: first_sum(i).wait_recv())
    zp[0] = zp_own[...]
    total = zp[z].astype(F32)
    for r in range(1, planes):
        total = total + zp[(z + planes - r) % planes].astype(F32)
    v[0, at(dp), :] = halves(fold(total))

    def spread(slot, i, owner):
        return remote(v.at[slot, at(owner)], v.at[slot, at(owner)], it_s.at[slot, i], it_r.at[slot, i], dp=peer(i))

    each(1, replicas, lambda i: spread(0, i, dp).start())

    each(1, replicas, lambda i: gather(i, source(i)).wait_recv())
    remote(own.at[1 - core], own.at[1 - core], own_sem.at[0], own_sem.at[1], row=1 - core).wait_recv()
    tile = 256

    def plane_term(i):
        here = pl.ds(pl.multiple_of(i * tile, tile), tile)
        for c in range(2):
            term = lax.dot_general(own[c], mz[here, :], NT, preferred_element_type=F32)
            kpart[c * part : (c + 1) * part, here] = term.astype(BF16)

    each(0, rows // tile, plane_term)

    def piece(ref, i):
        return ref.at[
            pl.ds(pl.multiple_of(i // 2 * quarter, quarter), quarter),
            pl.ds(pl.multiple_of(i % 2 * half, half), half),
        ]

    def k_scatter(i):
        return remote(piece(kpart, zpeer(i)), zbuf.at[i], z2_s.at[i], z2_r.at[i], col=zpeer(i))

    def k_gather(i, owner):
        return remote(piece(kfull, owner), piece(kfull, owner), z3_s.at[i], z3_r.at[i], col=zpeer(i))

    each(1, planes, lambda i: k_scatter(i).start())
    each(1, planes, lambda i: k_scatter(i).wait_recv())
    mine_rows, mine_cols = z // 2 * quarter, pl.ds(pl.multiple_of(z % 2 * half, half), half)

    def k_sum(i):
        here = pl.ds(pl.multiple_of(mine_rows + i * 16, 16), 16)
        total = kpart[here, mine_cols].astype(F32)
        for r in range(1, planes):
            total = total + zbuf[r, pl.ds(pl.multiple_of(i * 16, 16), 16), :].astype(F32)
        kfull[here, mine_cols] = total.astype(BF16)

    each(0, quarter // 16, k_sum)
    each(1, planes, lambda i: k_gather(i, z).start())
    each(1, planes, lambda i: k_gather(i, zsource(i)).wait_recv())

    eye = (lax.broadcasted_iota(jnp.int32, (128, 256), 0) % 64 == lanes((128, 256)) % 64) & (lanes((128, 256)) < 128)
    factor[...] = eye.astype(F32).astype(BF16)

    def apply(value):
        twice = jnp.concatenate([value, value], 1)
        return lax.dot_general(twice, factor[...], NT, preferred_element_type=F32)

    def swap_y(slot):
        return remote(ysend.at[slot], yrecv.at[slot], y_sem.at[0, slot], y_sem.at[1, slot], row=1 - core)

    def swap_gram(slot):
        return remote(gsend.at[slot], grecv.at[slot], gr_sem.at[0, slot], gr_sem.at[1, slot], row=1 - core)

    def iterate(k):
        slot, after = k % 2, (k + 1) % 2
        each(1, replicas, lambda i: spread(slot, i, source(i)).wait_recv())
        pp[...] = halves(apply(v[slot]))

        @pl.when(k < ITERS - 1)
        def _():
            theirs = pl.ds(pl.multiple_of((1 - core) * part, part), part)
            ysend[slot] = jnp.dot(kfull[theirs, :], pp[...], preferred_element_type=F32)
            swap_y(slot).start()

        gsend[slot] = lax.dot_general(pp[...], pp[...], TN, preferred_element_type=F32)
        swap_gram(slot).start()

        @pl.when(k < ITERS - 1)
        def _():
            ours = pl.ds(pl.multiple_of(core * part, part), part)
            term = jnp.dot(kfull[ours, :], pp[...], preferred_element_type=F32)
            swap_y(slot).wait_recv()
            v[after, at(dp), :] = halves(fold(term + yrecv[slot]))
            each(1, replicas, lambda i: spread(after, i, dp).start())

        swap_gram(slot).wait_recv()
        gram = fold(gsend[slot] + grecv[slot])
        factor[...] = inverse_factor(gram[:64] + gram[64:])
        swap_gram(slot).wait_send()
        each(1, replicas, lambda i: spread(slot, i, dp).wait_send())

        @pl.when(k < ITERS - 1)
        def _():
            swap_y(slot).wait_send()

    each(0, ITERS, iterate)

    plow[...] = apply(pp[...])[:, :64].astype(BF16)
    qsend[...] = lax.dot_general(plow[...], mz[...], TN, preferred_element_type=F32)
    swap_q = remote(qsend, qrecv, q_sem.at[0], q_sem.at[1], row=1 - core)
    swap_q.start()
    swap_q.wait_recv()
    q_t = qsend[...] + qrecv[...]
    qlow[...] = q_t.astype(BF16)
    qf_ref[...] = q_t.T

    def left_over(i):
        here = at(i)
        approx = jnp.dot(plow[here, :], qlow[...], preferred_element_type=F32)
        out_buf[here, :] = (merged[here, :].astype(F32) - approx).astype(BF16)
        pltpu.make_async_copy(out_buf.at[here], err_ref.at[0, here], o_sem.at[i]).start()

    each(0, replicas, left_over)

    swap_q.wait_send()
    swap_own.wait_send()
    each(1, replicas, lambda i: scatter(i).wait_send())
    each(1, replicas, lambda i: gather(i, dp).wait_send())
    each(1, planes, lambda i: first_sum(i).wait_send())
    each(1, planes, lambda i: k_scatter(i).wait_send())
    each(1, planes, lambda i: k_gather(i, z).wait_send())

    def stored(i):
        here = at(i)
        pltpu.make_async_copy(out_buf.at[here], err_ref.at[0, here], o_sem.at[i]).wait()

    each(0, replicas, stored)


def solution(mesh):
    replicas, planes = mesh.shape["dp"], mesh.shape["col"]

    def shards(grads, errors, q_init):
        _, rows, cols = grads.shape
        part = rows // replicas
        rank = q_init.shape[1]
        dma = pltpu.SemaphoreType.DMA
        whole = pltpu.VMEM((rows, cols), BF16)
        chip = 2 * part
        scratch = [
            whole, whole, whole,
            pltpu.VMEM((replicas, part, cols), BF16),
            whole,
            pltpu.VMEM((2, part, cols), BF16),
            pltpu.VMEM((chip, rows), BF16),
            pltpu.VMEM((chip, rows), BF16),
            pltpu.VMEM((planes, chip // 4, rows // 2), BF16),
            pltpu.VMEM((planes, part, 128), BF16),
            pltpu.VMEM((part, 128), BF16),
            pltpu.VMEM((2, rows, 128), BF16),
            pltpu.VMEM((rows, 128), BF16),
            pltpu.VMEM((128, 256), BF16),
            pltpu.VMEM((2, part, 128), F32), pltpu.VMEM((2, part, 128), F32),
            pltpu.VMEM((2, 128, 128), F32), pltpu.VMEM((2, 128, 128), F32),
            pltpu.VMEM((rank, cols), F32), pltpu.VMEM((rank, cols), F32),
            pltpu.VMEM((rank, cols), BF16),
            pltpu.VMEM((rows, rank), BF16),
            whole,
            dma((replicas,)), dma((replicas,)),
            dma((replicas,)), dma((replicas,)),
            dma((replicas,)), dma((replicas,)),
            dma((2,)),
            dma((planes,)), dma((planes,)), dma((planes,)), dma((planes,)), dma((planes,)), dma((planes,)),
            dma((2, replicas)), dma((2, replicas)),
            dma((2, 2)), dma((2, 2)), dma((2,)),
            dma((replicas,)),
        ]
        return pl.pallas_call(
            functools.partial(kernel, replicas, planes),
            out_shape=(
                jax.ShapeDtypeStruct(grads.shape, BF16),
                jax.ShapeDtypeStruct(q_init.shape, F32),
            ),
            in_specs=[pl.BlockSpec(memory_space=pl.ANY)] * 2 + [pl.BlockSpec(memory_space=pltpu.VMEM)],
            out_specs=(pl.BlockSpec(memory_space=pl.ANY), pl.BlockSpec(memory_space=pltpu.VMEM)),
            scratch_shapes=scratch,
            compiler_params=pltpu.CompilerParams(
                collective_id=0, has_side_effects=True, vmem_limit_bytes=48 * 2**20
            ),
            name="power_round",
        )(grads, errors, q_init)

    return jax.shard_map(
        shards,
        mesh=mesh,
        in_specs=(P("dp", "row", "col"), P("dp", "row", "col"), P("col", None)),
        out_specs=(P("dp", "row", "col"), P("col", None)),
        check_vma=False,
    )
```

```python
import functools

import jax
import jax.numpy as jnp
from jax import lax
from jax.experimental import pallas as pl
from jax.experimental.pallas import tpu as pltpu
from jax.sharding import PartitionSpec as P

MESH = pl.DeviceIdType.MESH
ITERS = 7
F32, BF16 = jnp.float32, jnp.bfloat16
NT = (((1,), (1,)), ((), ()))
TN = (((0,), (0,)), ((), ()))
SIDE = 4


def lanes(shape):
    return lax.broadcasted_iota(jnp.int32, shape, 1)


def halves(x):
    high = x.astype(BF16)
    low = (x - high.astype(F32)).astype(BF16)
    return jnp.where(lanes(x.shape) < 64, high, low)


def fold(x):
    return x + pltpu.roll(x, 64, 1)


def inverse_factor(gram):
    shape = (64, 128)
    lane, row = lanes(shape), lax.broadcasted_iota(jnp.int32, shape, 0)
    w = jnp.where(lane < 64, gram, (lane - 64 == row).astype(F32))
    for j in range(64):
        g = 8 * (j // 8)
        tail = w[g:]
        scale = tail[:, j : j + 1] * (1.0 / w[j : j + 1, j : j + 1])
        scale = jnp.where(row[g:, :1] > j, scale, 0.0)
        tail = tail - scale * w[j : j + 1]
        w = jnp.concatenate([w[:g], tail], 0) if g else tail
    pivot = jnp.sum(jnp.where(lane == row, w, 0.0), axis=1, keepdims=True)
    w = jnp.where(lane < 64, 0.0, w * lax.rsqrt(pivot))
    w = fold(w)
    high = w.astype(BF16)
    low = (w - high.astype(F32)).astype(BF16)
    both = jnp.concatenate([high, low], 1)
    return jnp.concatenate([both, both], 0)


def kernel(
    replicas, planes, g_ref, e_ref, q_ref, err_ref, qt_ref,
    g_buf, e_buf, merged, rsa, rsb, sa, sb, rs2a, rs2b, mz, own, kk, zbuf, zp, zown, v, pp, factor, ybuf, yrecv, ytot,
    gsend, grecv, qsend, qrecv, qlow, plow,
    g_sem, e_sem, rs_s, rs_r, ag_s, ag_r, own_sem, z1_s, z1_r, z2_s, z2_r, z3_s, z3_r, it_s, it_r, y_sem, gr_sem, q_sem,
):
    dp, core, z = lax.axis_index("dp"), lax.axis_index("row"), lax.axis_index("col")
    y, x = dp // SIDE, dp % SIDE
    _, _, part, cols = merged.shape
    rows = replicas * part
    first, second = pl.ds(0, cols // 2), pl.ds(cols // 2, cols // 2)
    half, quarter = rows // 2, 2 * part // 4

    def up(a, i):
        return (a + i) % SIDE

    def down(a, i):
        return (a + SIDE - i) % SIDE

    def at(i):
        return pl.ds(pl.multiple_of(i * part, part), part)

    def zpeer(i):
        return (z + i) % planes

    def zsource(i):
        return (z + planes - i) % planes

    def remote(src, dst, ssem, rsem, **device):
        return pltpu.make_async_remote_copy(
            src_ref=src, dst_ref=dst, send_sem=ssem, recv_sem=rsem, device_id=device, device_id_type=MESH
        )

    def each(lo, hi, body):
        def step(i, carry):
            body(i)
            return carry

        lax.fori_loop(lo, hi, step, 0)

    def loads(i):
        yi, xi = i % SIDE, up(x, i // SIDE + 1)
        here = at(yi * SIDE + xi)
        return (
            pltpu.make_async_copy(g_ref.at[0, here], g_buf.at[yi, xi], g_sem.at[i]),
            pltpu.make_async_copy(e_ref.at[0, here], e_buf.at[yi, xi], e_sem.at[i]),
        )

    def load(i):
        for copy in loads(i):
            copy.start()

    def peer(i):
        return up(y, i // SIDE) * SIDE + up(x, i % SIDE)

    def source(i):
        return down(y, i // SIDE) * SIDE + down(x, i % SIDE)

    each(0, replicas, load)
    barrier = pltpu.get_barrier_semaphore()
    each(1, replicas, lambda i: pl.semaphore_signal(barrier, inc=1, device_id={"dp": peer(i)}, device_id_type=MESH))
    each(1, planes, lambda i: pl.semaphore_signal(barrier, inc=1, device_id={"col": zpeer(i)}, device_id_type=MESH))
    pl.semaphore_signal(barrier, inc=1, device_id={"row": 1 - core}, device_id_type=MESH)
    pl.semaphore_wait(barrier, replicas - 1 + planes - 1 + 1)

    def scatter_a(i):
        to = up(x, i)
        return remote(merged.at[:, to, :, first], rsa.at[i], rs_s.at[0, i], rs_r.at[0, i], dp=y * SIDE + to)

    def scatter_b(i):
        to = up(y, i)
        return remote(merged.at[to, :, :, second], rsb.at[i], rs_s.at[1, i], rs_r.at[1, i], dp=to * SIDE + x)

    def merge(i):
        yi, xi = i % SIDE, up(x, i // SIDE + 1)
        for copy in loads(i):
            copy.wait()
        merged[yi, xi] = (g_buf[yi, xi].astype(F32) + e_buf[yi, xi].astype(F32)).astype(BF16)

    def merge_send(i):
        each((i - 1) * SIDE, i * SIDE, merge)
        scatter_a(i).start()

    each(1, SIDE, merge_send)
    each((SIDE - 1) * SIDE, SIDE * SIDE, merge)
    each(1, SIDE, lambda i: scatter_b(i).start())

    def scatter_a2(i):
        return remote(sa.at[i], rs2a.at[i], rs_s.at[2, i], rs_r.at[2, i], dp=up(y, i) * SIDE + x)

    def scatter_b2(i):
        return remote(sb.at[i], rs2b.at[i], rs_s.at[3, i], rs_r.at[3, i], dp=y * SIDE + up(x, i))

    def four_a(to):
        total = merged[to, x, :, first].astype(F32)
        for r in range(1, SIDE):
            total = total + rsa[r, to].astype(F32)
        return total

    def four_b(to):
        total = merged[y, to, :, second].astype(F32)
        for r in range(1, SIDE):
            total = total + rsb[r, to].astype(F32)
        return total

    def send_a(i):
        sa[i] = four_a(up(y, i)).astype(BF16)
        scatter_a2(i).start()

    def send_b(i):
        sb[i] = four_b(up(x, i)).astype(BF16)
        scatter_b2(i).start()

    each(1, SIDE, lambda i: scatter_a(i).wait_recv())
    each(1, SIDE, send_a)
    each(1, SIDE, lambda i: scatter_b(i).wait_recv())
    each(1, SIDE, send_b)

    def mean(total, others, columns):
        for r in range(1, SIDE):
            total = total + others[r].astype(F32)
        low = (total * (1.0 / replicas)).astype(BF16)
        mz[y, x, :, columns] = low
        own[core, :, columns] = low

    def gather_a(i, xi):
        block = mz.at[y, xi, :, first]
        return remote(block, block, ag_s.at[0, i], ag_r.at[0, i], dp=y * SIDE + up(x, i))

    def gather_b(i, yi):
        block = mz.at[yi, x, :, second]
        return remote(block, block, ag_s.at[1, i], ag_r.at[1, i], dp=up(y, i) * SIDE + x)

    def gather_a2(i, yi):
        block = mz.at[yi, :, :, first]
        return remote(block, block, ag_s.at[2, i], ag_r.at[2, i], dp=up(y, i) * SIDE + x)

    def gather_b2(i, xi):
        block = mz.at[:, xi, :, second]
        return remote(block, block, ag_s.at[3, i], ag_r.at[3, i], dp=y * SIDE + up(x, i))

    total = four_a(y)
    each(1, SIDE, lambda i: scatter_a2(i).wait_recv())
    mean(total, rs2a, first)
    each(1, SIDE, lambda i: gather_a(i, x).start())
    total = four_b(x)
    each(1, SIDE, lambda i: scatter_b2(i).wait_recv())
    mean(total, rs2b, second)
    each(1, SIDE, lambda i: gather_b(i, y).start())
    swap_own = remote(own.at[core], own.at[core], own_sem.at[0], own_sem.at[1], row=1 - core)
    swap_own.start()

    def z_copy(which, i):
        return remote(zown.at[which], zp.at[which, i], z1_s.at[which, i], z1_r.at[which, i], col=zpeer(i))

    def z_send(which, term):
        zown[which] = halves(term)
        each(1, planes, lambda i: z_copy(which, i).start())

    def z_total(which):
        each(1, planes, lambda i: z_copy(which, i).wait_recv())
        zp[which, 0] = zown[which]
        total = zp[which, z].astype(F32)
        for r in range(1, planes):
            total = total + zp[which, (z + planes - r) % planes].astype(F32)
        return fold(total)

    def spread(slot, i, owner):
        return remote(v.at[slot, at(owner)], v.at[slot, at(owner)], it_s.at[slot, i], it_r.at[slot, i], dp=peer(i))

    term = lax.dot_general(own[core], q_ref[...].astype(BF16), NT, preferred_element_type=F32)
    z_send(0, jnp.concatenate([term, term], 1))
    each(1, SIDE, lambda i: gather_a(i, down(x, i)).wait_recv())
    each(1, SIDE, lambda i: gather_a2(i, y).start())
    each(1, SIDE, lambda i: gather_b(i, down(y, i)).wait_recv())
    each(1, SIDE, lambda i: gather_b2(i, x).start())
    v[0, at(dp), :] = halves(z_total(0))
    each(1, replicas, lambda i: spread(0, i, dp).start())

    remote(own.at[1 - core], own.at[1 - core], own_sem.at[0], own_sem.at[1], row=1 - core).wait_recv()
    each(1, SIDE, lambda i: gather_a2(i, down(y, i)).wait_recv())
    each(1, SIDE, lambda i: gather_b2(i, down(x, i)).wait_recv())
    tile = SIDE * part

    def plane_term(i):
        block = mz[i].reshape(tile, cols)
        for c in range(2):
            term = lax.dot_general(own[c], block, NT, preferred_element_type=F32)
            kk[0, c * part : (c + 1) * part, pl.ds(pl.multiple_of(i * tile, tile), tile)] = term.astype(BF16)

    each(0, SIDE, plane_term)

    def piece(which, i):
        return kk.at[
            which,
            pl.ds(pl.multiple_of(i // 2 * quarter, quarter), quarter),
            pl.ds(pl.multiple_of(i % 2 * half, half), half),
        ]

    def k_scatter(i):
        return remote(piece(0, zpeer(i)), zbuf.at[i], z2_s.at[i], z2_r.at[i], col=zpeer(i))

    def k_gather(i, owner):
        return remote(piece(1, owner), piece(1, owner), z3_s.at[i], z3_r.at[i], col=zpeer(i))

    def k_sum(i):
        here = pl.ds(pl.multiple_of(z // 2 * quarter + i * 16, 16), 16)
        mine = pl.ds(pl.multiple_of(z % 2 * half, half), half)
        total = kk[0, here, mine].astype(F32)
        for r in range(1, planes):
            total = total + zbuf[r, pl.ds(pl.multiple_of(i * 16, 16), 16), :].astype(F32)
        kk[1, here, mine] = total.astype(BF16)

    each(1, planes, lambda i: k_scatter(i).start())

    eye = (lax.broadcasted_iota(jnp.int32, (128, 256), 0) % 64 == lanes((128, 256)) % 64) & (lanes((128, 256)) < 128)
    factor[...] = eye.astype(F32).astype(BF16)

    def apply(value):
        twice = jnp.concatenate([value, value], 1)
        return lax.dot_general(twice, factor[...], NT, preferred_element_type=F32)

    def swap_y(slot):
        return remote(ybuf.at[1 - core], yrecv.at[slot], y_sem.at[0, slot], y_sem.at[1, slot], row=1 - core)

    def swap_gram(slot):
        return remote(gsend, grecv.at[slot], gr_sem.at[0, slot], gr_sem.at[1, slot], row=1 - core)

    swap_q = remote(qsend, qrecv, q_sem.at[0], q_sem.at[1], row=1 - core)

    def iterate(k):
        slot, after = k % 2, (k + 1) % 2
        each(1, replicas, lambda i: spread(slot, i, source(i)).wait_recv())
        pp[...] = halves(apply(v[slot]))

        @pl.when(k == 1)
        def _():
            each(1, planes, lambda i: k_gather(i, zsource(i)).wait_recv())

        @pl.when(k < ITERS - 1)
        def _():
            which = (k + ITERS - 1) // ITERS
            ybuf[...] = jnp.dot(kk[which], pp[...], preferred_element_type=F32).reshape(ybuf.shape)
            swap_y(slot).start()

        gsend[...] = lax.dot_general(pp[...], pp[...], TN, preferred_element_type=F32)
        swap_gram(slot).start()

        @pl.when(k < ITERS - 1)
        def _():
            swap_y(slot).wait_recv()
            ytot[...] = fold(ybuf[core] + yrecv[slot])

        @pl.when(k == 0)
        def _():
            z_send(1, ytot[...])
            ytot[...] = z_total(1)

        @pl.when(k < ITERS - 1)
        def _():
            v[after, at(dp), :] = halves(ytot[...])
            each(1, replicas, lambda i: spread(after, i, dp).start())

        @pl.when(k == 0)
        def _():
            each(1, planes, lambda i: k_scatter(i).wait_recv())
            each(0, quarter // 16, k_sum)
            each(1, planes, lambda i: k_gather(i, z).start())

        @pl.when(k == ITERS - 1)
        def _():
            both = lax.dot_general(pp[...], mz[...].reshape(rows, cols), TN, preferred_element_type=F32)
            qsend[...] = both[:64] + both[64:]
            swap_q.start()

        swap_gram(slot).wait_recv()
        gram = fold(gsend[...] + grecv[slot])
        factor[...] = inverse_factor(gram[:64] + gram[64:])
        swap_gram(slot).wait_send()
        each(1, replicas, lambda i: spread(slot, i, dp).wait_send())

        @pl.when(k < ITERS - 1)
        def _():
            swap_y(slot).wait_send()

    each(0, ITERS, iterate)

    swap_q.wait_recv()
    q_t = qsend[...] + qrecv[...]
    high = q_t.astype(BF16)
    low = (q_t - high.astype(F32)).astype(BF16)
    q_t = jnp.dot(factor[:64, :], jnp.concatenate([high, low, high, low], 0), preferred_element_type=F32)
    qt_ref[...] = q_t
    qlow[...] = q_t.astype(BF16)
    plow[...] = apply(pp[...])[:, :64].astype(BF16)

    def left_over(i):
        approx = jnp.dot(plow[at(i), :], qlow[...], preferred_element_type=F32)
        err_ref[0, at(i), :] = (merged[i // SIDE, i % SIDE].astype(F32) - approx).astype(BF16)

    each(0, replicas, left_over)

    swap_q.wait_send()
    swap_own.wait_send()

    def sent(i):
        for copy in (scatter_a(i), scatter_b(i), scatter_a2(i), scatter_b2(i)):
            copy.wait_send()
        for copy in (gather_a(i, x), gather_b(i, y), gather_a2(i, y), gather_b2(i, x)):
            copy.wait_send()

    def sent_z(i):
        for copy in (z_copy(0, i), z_copy(1, i), k_scatter(i), k_gather(i, z)):
            copy.wait_send()

    each(1, SIDE, sent)
    each(1, planes, sent_z)


def solution(mesh):
    replicas, planes = mesh.shape["dp"], mesh.shape["col"]

    def shards(grads, errors, q_init):
        _, rows, cols = grads.shape
        part = rows // replicas
        rank = q_init.shape[1]
        dma = pltpu.SemaphoreType.DMA
        blocks = pltpu.VMEM((SIDE, SIDE, part, cols), BF16)
        line = pltpu.VMEM((SIDE, SIDE, part, cols // 2), BF16)
        single = pltpu.VMEM((SIDE, part, cols // 2), BF16)
        p_f32 = pltpu.VMEM((part, 128), F32)
        chip = 2 * part
        scratch = [
            blocks, blocks, blocks,
            line, line, single, single, single, single,
            blocks,
            pltpu.VMEM((2, part, cols), BF16),
            pltpu.VMEM((2, chip, rows), BF16),
            pltpu.VMEM((planes, chip // 4, rows // 2), BF16),
            pltpu.VMEM((2, planes, part, 128), BF16),
            pltpu.VMEM((2, part, 128), BF16),
            pltpu.VMEM((2, rows, 128), BF16),
            pltpu.VMEM((rows, 128), BF16),
            pltpu.VMEM((128, 256), BF16),
            pltpu.VMEM((2, part, 128), F32), pltpu.VMEM((2, part, 128), F32), p_f32,
            pltpu.VMEM((128, 128), F32), pltpu.VMEM((2, 128, 128), F32),
            pltpu.VMEM((rank, cols), F32), pltpu.VMEM((rank, cols), F32),
            pltpu.VMEM((rank, cols), BF16),
            pltpu.VMEM((rows, rank), BF16),
            dma((replicas,)), dma((replicas,)),
            dma((4, SIDE)), dma((4, SIDE)), dma((4, SIDE)), dma((4, SIDE)),
            dma((2,)),
            dma((2, planes)), dma((2, planes)), dma((planes,)), dma((planes,)), dma((planes,)), dma((planes,)),
            dma((2, replicas)), dma((2, replicas)),
            dma((2, 2)), dma((2, 2)), dma((2,)),
        ]
        vmem = pl.BlockSpec(memory_space=pltpu.VMEM)
        new_errors, q_t = pl.pallas_call(
            functools.partial(kernel, replicas, planes),
            out_shape=(
                jax.ShapeDtypeStruct(grads.shape, BF16),
                jax.ShapeDtypeStruct((rank, cols), F32),
            ),
            in_specs=[pl.BlockSpec(memory_space=pl.ANY)] * 2 + [vmem],
            out_specs=(vmem, vmem),
            scratch_shapes=scratch,
            compiler_params=pltpu.CompilerParams(
                collective_id=0, has_side_effects=True, vmem_limit_bytes=48 * 2**20
            ),
            name="power_round",
        )(grads, errors, q_init.T)
        return new_errors, q_t.T

    return jax.shard_map(
        shards,
        mesh=mesh,
        in_specs=(P("dp", "row", "col"), P("dp", "row", "col"), P("col", None)),
        out_specs=(P("dp", "row", "col"), P("col", None)),
        check_vma=False,
    )
```
